32 devices in a mesh: tau: 2 (over x), basis: 16 (over z, y, core).
Axes of the slice: x: 2, y: 2, z: 4, core: 2. Of those that a mesh axis runs over, the one named last changes fastest.
Arguments:
- three_center: bfloat16 [64, 512, 512], P(None, 'basis'), may hold values from -6 to 6
- tensor_mask: int32 [64, 32, 32], P(None, 'basis'), may hold values 0 or 1
- occupied_green: bfloat16 [1024, 512], P(('tau', 'basis')), parts along dimension 0, may hold values from -0.75 to 0.75
- occupied_mask: int32 [64, 32], P(('tau', 'basis')), parts along dimension 0, may hold values 0 or 1
- virtual_green: bfloat16 [1024, 512], P(('tau', 'basis')), parts along dimension 0, may hold values from -0.75 to 0.75
- virtual_mask: int32 [64, 32], P(('tau', 'basis')), parts along dimension 0, may hold values 0 or 1
- atom_size: int32 [32], replicated, may hold values from 8 to 16, as said below
- auxiliary_owner: int32 [64], replicated, may hold values from 0 to 63, each once
Outputs:
- chi_owned: float32 [128, 64], P(('tau', 'basis')), parts along dimension 0
The draws below stay inside these ranges and needn't reach their ends.
There are 2 independent parts, one for each index of `tau`. The reference program is written for one: setup_inputs(seed, part) draws one part's arguments, and reference() takes and returns one part's arrays. A program takes and returns all parts, laid end to end along the dimension named above; an argument that names none is the same for every part. Nothing has to cross between parts.
Inputs may be any that keep to these rules, and one draw needn't show every extreme that they name: `atom_size`: each atom block holds 8 to 16 live functions; some block holds exactly 16 and some exactly 8. `auxiliary_owner`: A permutation of the auxiliary functions.
All inputs are finite; a program needn't handle non-finite values. No bound on the sum of `tensor_mask` or of `occupied_mask` or of `virtual_mask` on one device may be relied on, other than what follows from the above.
Results may differ from the reference program's by a relative error of at most 0.0041.
Values may be sent and summed in bfloat16 or wider, within the bound.
A program may use at most 128 MiB of HBM per device.

```python
import jax
import jax.numpy as jnp
from jax import lax

FA = 16
NATOM = 32
NB = 512
NP = 64


def draw_atom_size(key, part):
    key = jax.random.fold_in(key, 7)
    size_key, pick_key = jax.random.split(key)
    sizes = jax.random.randint(size_key, (NATOM,), FA // 2, FA + 1)
    picked = jax.random.permutation(pick_key, NATOM)
    sizes = sizes.at[picked[0]].set(FA).at[picked[1]].set(FA // 2)
    return sizes.astype(jnp.int32)


def set_ends(entries, stream_key, least, top_value):
    index_at = [jax.random.randint(jax.random.fold_in(stream_key, axis), (), 0, length) for axis, length in enumerate(entries.shape)]
    longest = entries.shape.index(max(entries.shape))
    next_to = index_at[:longest] + [(index_at[longest] + 1) % entries.shape[longest]] + index_at[longest + 1:]
    return entries.at[tuple(index_at)].set(least).at[tuple(next_to)].set(top_value)


def shard_levels(rng, dims, pieces, least, largest):
    def one(axis_at, parts):
        draws = jax.random.uniform(jax.random.fold_in(jax.random.fold_in(rng, 6), axis_at), (parts,), jnp.float32, least / len(pieces), largest / len(pieces))
        return jnp.repeat(jnp.exp(draws), dims[axis_at] // parts).reshape((-1,) + (1,) * (len(dims) - axis_at - 1))

    level = one(*pieces[0])
    for cut in pieces[1:]:
        level = level * one(*cut)
    return level


def scatter_about(rng, shape, spread, reach, pieces=(), held_as=jnp.bfloat16):
    entries = jax.random.normal(rng, shape, jnp.float32) * spread
    if len(pieces) > 0:
        entries = shard_levels(rng, shape, pieces, -0.22, 0.18) * entries
    return jnp.clip(entries, min=-reach, max=reach).astype(held_as)


def setup_inputs(seed: int = 0, part: int = 0) -> dict:
    splits = jax.random.split(jax.random.key(seed), 9)
    own_keys = jax.random.split(jax.random.fold_in(splits[8], part), 9)
    three_center = scatter_about(splits[0], (NP, NB, NB), 1.0, 6.0, ((1, 16),))
    tensor_mask = set_ends((jax.random.randint(splits[1], (NP, NATOM, NATOM), 0, 2) < 1).astype(jnp.int32), jax.random.fold_in(splits[1], 1), 0, 1)
    occupied_green = scatter_about(own_keys[2], (NB, NB), (NB // 8) ** -0.5, 0.75, ((0, 16),))
    occupied_mask = set_ends((jax.random.randint(own_keys[3], (NATOM, NATOM), 0, 3) < 2).astype(jnp.int32), jax.random.fold_in(own_keys[3], 1), 0, 1)
    virtual_green = scatter_about(own_keys[4], (NB, NB), (NB // 8) ** -0.5, 0.75, ((0, 16),))
    virtual_mask = set_ends((jax.random.randint(own_keys[5], (NATOM, NATOM), 0, 3) < 2).astype(jnp.int32), jax.random.fold_in(own_keys[5], 1), 0, 1)
    atom_size = draw_atom_size(jax.random.fold_in(splits[8], 71), part)
    auxiliary_owner = jax.random.permutation(splits[7], NP).astype(jnp.int32)
    return {"three_center": three_center, "tensor_mask": tensor_mask, "occupied_green": occupied_green, "occupied_mask": occupied_mask, "virtual_green": virtual_green, "virtual_mask": virtual_mask, "atom_size": atom_size, "auxiliary_owner": auxiliary_owner}


def alive_functions(atom_size):
    within = jnp.arange(FA, dtype=jnp.int32)[None, :] < atom_size[:, None]
    return within.astype(jnp.float32).reshape(-1)


def spread_blocks(block_mask):
    return jnp.repeat(jnp.repeat(block_mask, FA, axis=0), FA, axis=1).astype(jnp.float32)


def masked_matrix(matrix, block_mask, alive):
    factor = spread_blocks(block_mask) * alive[:, None] * alive[None, :]
    return (matrix.astype(jnp.float32) * factor).astype(jnp.bfloat16)


def reference(three_center, tensor_mask, occupied_green, occupied_mask, virtual_green, virtual_mask, atom_size, auxiliary_owner):
    alive = alive_functions(atom_size)
    occupied = masked_matrix(occupied_green, occupied_mask, alive)
    virtual = masked_matrix(virtual_green, virtual_mask, alive)

    def one_function(operands):
        tensor_slice, mask_slice = operands
        masked = masked_matrix(tensor_slice, mask_slice, alive)
        half_term = jnp.dot(masked, virtual.T, preferred_element_type=jnp.float32).astype(jnp.bfloat16)
        response = jnp.dot(occupied, half_term, preferred_element_type=jnp.float32).astype(jnp.bfloat16)
        return masked, response

    masked_three, responses = lax.map(one_function, (three_center, tensor_mask))
    flat_three = masked_three.reshape(NP, -1)
    flat_response = responses.reshape(NP, -1)
    chi = jnp.dot(flat_three, flat_response.T, preferred_element_type=jnp.float32) * (1.0 / NB)
    return jnp.zeros((NP, NP), jnp.float32).at[auxiliary_owner].set(chi)
```

```python
import functools

import jax
import jax.numpy as jnp
from jax import lax
from jax.experimental import pallas as pl
from jax.experimental.pallas import tpu as pltpu
from jax.sharding import PartitionSpec as P

FA = 16
LANES = 128
GROUPS = 4
BF = jnp.bfloat16
F32 = jnp.float32


def wait_for(ref, sem):
    pltpu.make_async_copy(ref, ref, sem).wait()


def one_hot(cond):
    return jnp.where(cond, 1.0, 0.0).astype(F32)


def kernel(
    n,
    t_hbm,
    tmask_ref,
    og_ref,
    om_ref,
    vg_ref,
    vm_ref,
    size_ref,
    owner_ref,
    out_ref,
    tm,
    st,
    sh,
    rt,
    rh,
    vf,
    of,
    vt,
    perm,
    factor,
    chi,
    route,
    csend,
    crecv,
    load_sem,
    own_sem,
    small_send,
    small_recv,
    t_send,
    t_recv,
    h_send,
    h_recv,
    c_send,
    c_recv,
):
    me = lax.axis_index("basis")
    tau = lax.axis_index("tau")
    aux, width, basis = tm.shape
    pack = LANES // width
    groups = aux // pack
    steps = groups // GROUPS
    chunks = basis // LANES
    atoms = basis // FA
    row_atoms = width // FA
    wide = pack * LANES
    block_rows = GROUPS * width
    owned = aux // n
    pad_rows = csend.shape[1]

    def peer_of(k):
        return lax.rem(me + k, n)

    def each_peer(body):
        def step(k, carry):
            body(peer_of(k))
            return carry

        lax.fori_loop(1, n, step, 0)

    def target(peer):
        return dict(device_id=(tau, peer), device_id_type=pl.DeviceIdType.MESH)

    barrier = pltpu.get_barrier_semaphore()
    each_peer(lambda peer: pl.semaphore_signal(barrier, inc=1, **target(peer)))
    load = pltpu.make_async_copy(t_hbm, tm, load_sem)
    load.start()

    lane = lax.broadcasted_iota(jnp.int32, (1, basis), 1)
    live = jnp.zeros((1, basis), F32)
    for a in range(atoms):
        hit = (lane >= a * FA) & (lane < a * FA + size_ref[a])
        live = live + one_hot(hit)
    atom_row = lax.broadcasted_iota(jnp.int32, (atoms, basis), 0)
    atom_lane = lax.broadcasted_iota(jnp.int32, (atoms, basis), 1) // FA
    spread = (one_hot(atom_row == atom_lane) * live).astype(BF)
    within = lax.broadcasted_iota(jnp.int32, (FA, basis), 0)
    live_rows = [one_hot(within < size_ref[me * row_atoms + a]) for a in range(row_atoms)]

    def factors(mask):
        return jnp.dot(mask.astype(F32).astype(BF), spread, preferred_element_type=F32)

    def masked_rows(rows_ref, mask_ref):
        f = factors(mask_ref[...])
        parts = [
            rows_ref[a * FA : (a + 1) * FA, :].astype(F32) * (f[a : a + 1, :] * live_rows[a])
            for a in range(row_atoms)
        ]
        return jnp.concatenate(parts, axis=0).astype(BF)

    vf[me] = masked_rows(vg_ref, vm_ref)
    of[me] = masked_rows(og_ref, om_ref)
    pl.semaphore_wait(barrier, n - 1)

    def send_small(peer):
        for i, ref in enumerate((vf, of)):
            pltpu.make_async_remote_copy(
                ref.at[me], ref.at[me], small_send.at[i], small_recv.at[i], **target(peer)
            ).start()

    each_peer(send_small)

    for a in range(row_atoms):
        factor[a] = factors(tmask_ref[:, a, :])
    src = lax.broadcasted_iota(jnp.int32, (wide, wide), 0)
    dst = lax.broadcasted_iota(jnp.int32, (wide, wide), 1)
    same = (src // LANES == (dst % LANES) // width) & ((src % LANES) // width == dst // LANES)
    perm[...] = one_hot(same & (src % width == dst % width)).astype(BF)
    load.wait()

    def shuffle(parts, out, q):
        stacked = jnp.concatenate(
            [
                jnp.concatenate([x[:, c * LANES : (c + 1) * LANES] for x in parts], axis=1)
                for c in range(chunks)
            ],
            axis=0,
        )
        moved = jnp.dot(stacked, perm[...], preferred_element_type=F32).astype(BF)
        for c in range(chunks):
            for i in range(pack):
                piece = moved[
                    c * block_rows : (c + 1) * block_rows, i * LANES : (i + 1) * LANES
                ]
                out[c * pack + i, pl.ds(q * GROUPS, GROUPS)] = piece.reshape(GROUPS, width, LANES)

    def send_step(out, into, q, send_sem, recv_sem):
        here = pl.ds(q * GROUPS, GROUPS)

        def send(peer):
            pltpu.make_async_remote_copy(
                out.at[peer, here], into.at[me, here], send_sem, recv_sem, **target(peer)
            ).start()

        each_peer(send)

    def tensor_step(q, carry):
        parts = []
        for j in range(pack):
            rows = []
            for r in range(GROUPS):
                p = j * groups + q * GROUPS + r
                f = [factor[a, pl.ds(p, 1), :] * live_rows[a] for a in range(row_atoms)]
                value = (tm[p].astype(F32) * jnp.concatenate(f, axis=0)).astype(BF)
                tm[p] = value
                rows.append(value)
            parts.append(jnp.concatenate(rows, axis=0))
        shuffle(parts, st, q)
        send_step(st, rt, q, t_send, t_recv)
        return carry

    lax.fori_loop(0, steps, tensor_step, 0)
    own_t = pltpu.make_async_copy(st.at[me], rt.at[me], own_sem.at[0])
    own_t.start()

    wait_for(vf.at[pl.ds(0, n - 1)], small_recv.at[0])
    vt[...] = vf[...].reshape(basis, basis).T

    def half_step(q, carry):
        rows = [
            tm[pl.ds(j * groups + q * GROUPS, GROUPS)].reshape(block_rows, basis)
            for j in range(pack)
        ]
        half = jnp.dot(
            jnp.concatenate(rows, axis=0), vt[...], preferred_element_type=F32
        ).astype(BF)
        shuffle([half[j * block_rows : (j + 1) * block_rows] for j in range(pack)], sh, q)
        send_step(sh, rh, q, h_send, h_recv.at[q])
        return carry

    lax.fori_loop(0, steps, half_step, 0)
    own_h = pltpu.make_async_copy(sh.at[me], rh.at[me], own_sem.at[1])
    own_h.start()

    slot = lax.broadcasted_iota(jnp.int32, (n * pad_rows, aux), 0)
    wanted = jnp.where(slot % pad_rows < owned, (slot // pad_rows) * owned + slot % pad_rows, -1)
    by_p = one_hot(wanted == owner_ref[...]).astype(BF)
    p_row = lax.broadcasted_iota(jnp.int32, (aux, aux), 0)
    p_col = lax.broadcasted_iota(jnp.int32, (aux, aux), 1)
    reorder = one_hot(p_row == (p_col % pack) * groups + p_col // pack).astype(BF)
    route[...] = jnp.dot(by_p, reorder, preferred_element_type=F32)
    chi[...] = jnp.zeros_like(chi)

    wait_for(of.at[pl.ds(0, n - 1)], small_recv.at[1])
    own_t.wait()
    wait_for(rt.at[pl.ds(0, n - 1)], t_recv)

    def turn(g, carry):
        tm[pl.ds(g * pack, pack)] = rt[:, g].reshape(basis, LANES).T.reshape(pack, width, basis)
        return carry

    lax.fori_loop(0, groups, turn, 0)
    own_h.wait()

    lanes = GROUPS * LANES
    diag = one_hot(
        lax.broadcasted_iota(jnp.int32, (width, lanes), 0)
        == lax.broadcasted_iota(jnp.int32, (width, lanes), 1) % width
    )
    b_row = lax.broadcasted_iota(jnp.int32, (lanes, chi.shape[1]), 0)
    b_col = lax.broadcasted_iota(jnp.int32, (lanes, chi.shape[1]), 1)
    place = (b_row % LANES) // width * groups + b_row // LANES

    def chi_step(q, carry):
        here = pl.ds(q * GROUPS, GROUPS)
        wait_for(rh.at[pl.ds(0, n - 1), here], h_recv.at[q])
        half = jnp.concatenate(
            [rh[:, q * GROUPS + r].reshape(basis, LANES) for r in range(GROUPS)], axis=1
        )
        response = jnp.dot(
            of[...].reshape(basis, basis), half, preferred_element_type=F32
        ).astype(BF)
        gather = one_hot(b_col == place + q * GROUPS)

        tile = GROUPS * pack
        for t in range(steps):
            left = tm[t * tile : (t + 1) * tile].reshape(tile * width, basis)
            both = jnp.dot(left, response, preferred_element_type=F32)
            traced = jnp.sum(both.reshape(tile, width, lanes) * diag[None], axis=1)
            chi[t * tile : (t + 1) * tile, :] += jnp.dot(
                traced, gather, precision=lax.Precision.HIGHEST, preferred_element_type=F32
            )
        return carry

    lax.fori_loop(0, steps, chi_step, 0)

    routed = jnp.dot(
        route[...], chi[...], precision=lax.Precision.HIGHEST, preferred_element_type=F32
    )
    csend[...] = routed.reshape(csend.shape)
    crecv[me] = csend[me]

    def send_chi(peer):
        pltpu.make_async_remote_copy(
            csend.at[peer], crecv.at[me], c_send, c_recv, **target(peer)
        ).start()

    each_peer(send_chi)
    wait_for(crecv.at[pl.ds(0, n - 1)], c_recv)
    total = jnp.sum(crecv[...], axis=0) * (1.0 / basis)
    out_ref[...] = total[:owned, :aux]

    wait_for(vf.at[pl.ds(0, n - 1)], small_send.at[0])
    wait_for(of.at[pl.ds(0, n - 1)], small_send.at[1])
    wait_for(st.at[pl.ds(0, n - 1)], t_send)
    wait_for(sh.at[pl.ds(0, n - 1)], h_send)
    wait_for(csend.at[pl.ds(0, n - 1)], c_send)


def local(
    n,
    three_center,
    tensor_mask,
    occupied_green,
    occupied_mask,
    virtual_green,
    virtual_mask,
    atom_size,
    auxiliary_owner,
):
    aux, width, basis = three_center.shape
    pack = LANES // width
    groups = aux // pack
    steps = groups // GROUPS
    wide = pack * LANES
    owned = aux // n
    pad_rows = -(-owned // 8) * 8
    cols = -(-aux // LANES) * LANES
    vmem = pl.BlockSpec(memory_space=pltpu.VMEM)
    exchanged = (n, groups, width, LANES)
    dma = pltpu.SemaphoreType.DMA
    return pl.pallas_call(
        functools.partial(kernel, n),
        out_shape=jax.ShapeDtypeStruct((owned, aux), F32),
        in_specs=[pl.BlockSpec(memory_space=pl.ANY)]
        + [vmem] * 5
        + [pl.BlockSpec(memory_space=pltpu.SMEM), vmem],
        out_specs=vmem,
        scratch_shapes=[
            pltpu.VMEM((aux, width, basis), BF),
            pltpu.VMEM(exchanged, BF),
            pltpu.VMEM(exchanged, BF),
            pltpu.VMEM(exchanged, BF),
            pltpu.VMEM(exchanged, BF),
            pltpu.VMEM((n, width, basis), BF),
            pltpu.VMEM((n, width, basis), BF),
            pltpu.VMEM((basis, basis), BF),
            pltpu.VMEM((wide, wide), BF),
            pltpu.VMEM((width // FA, aux, basis), F32),
            pltpu.VMEM((aux, cols), F32),
            pltpu.VMEM((n * pad_rows, aux), F32),
            pltpu.VMEM((n, pad_rows, cols), F32),
            pltpu.VMEM((n, pad_rows, cols), F32),
            dma,
            dma((2,)),
            dma((2,)),
            dma((2,)),
            dma,
            dma,
            dma,
            dma((steps,)),
            dma,
            dma,
        ],
        compiler_params=pltpu.CompilerParams(
            collective_id=0, has_side_effects=True, vmem_limit_bytes=60 * 1024 * 1024
        ),
    )(
        three_center,
        tensor_mask,
        occupied_green,
        occupied_mask,
        virtual_green,
        virtual_mask,
        atom_size,
        auxiliary_owner.reshape(1, aux),
    )


def solution(mesh):
    placed = (
        P(None, "basis", None),
        P(None, "basis", None),
        P(("tau", "basis"), None),
        P(("tau", "basis"), None),
        P(("tau", "basis"), None),
        P(("tau", "basis"), None),
        P(),
        P(),
    )
    return jax.shard_map(
        functools.partial(local, mesh.shape["basis"]),
        mesh=mesh,
        in_specs=placed,
        out_specs=P(("tau", "basis"), None),
        check_vma=False,
    )
```

```python
import functools

import jax
import jax.numpy as jnp
from jax import lax
from jax.experimental import pallas as pl
from jax.experimental.pallas import tpu as pltpu
from jax.sharding import PartitionSpec as P

FA = 16
LANES = 128
GROUPS = 2
BF = jnp.bfloat16
F32 = jnp.float32


def wait_for(ref, sem):
    pltpu.make_async_copy(ref, ref, sem).wait()


def one_hot(cond):
    return jnp.where(cond, 1.0, 0.0).astype(F32)


def kernel(
    n,
    parts,
    t_hbm,
    tmask_ref,
    og_ref,
    om_ref,
    vg_ref,
    vm_ref,
    size_ref,
    owner_ref,
    out_ref,
    tm,
    st,
    sh,
    rt,
    rh,
    vown,
    vf,
    of,
    vt,
    perm_t,
    perm_h,
    factor,
    chi,
    route,
    csend,
    crecv,
    cmine,
    cother,
    load_sem,
    own_sem,
    v_send,
    v_recv,
    o_send,
    o_recv,
    t_send,
    t_recv,
    h_send,
    h_recv,
    c_send,
    c_recv,
):
    me = lax.axis_index("basis")
    tau = lax.axis_index("tau")
    aux, width, basis = tm.shape
    share = width // parts
    pack = LANES // share
    groups = aux // pack
    steps = groups // GROUPS
    atoms = basis // FA
    row_atoms = width // FA
    rows = GROUPS * width
    owned = aux // n
    high = n // 4
    h_me, m_me, c_me = me // 4, (me // 2) % 2, me % 2

    def peer_of(k):
        return lax.rem(me + k, n)

    def each_peer(body):
        def step(k, carry):
            body(peer_of(k))
            return carry

        lax.fori_loop(1, n, step, 0)

    def at(part, place):
        return dict(device_id=(part, place), device_id_type=pl.DeviceIdType.MESH)

    def send(src, dst, send_sem, recv_sem, part, place):
        pltpu.make_async_remote_copy(src, dst, send_sem, recv_sem, **at(part, place)).start()

    other_parts = [lax.rem(tau + k, parts) for k in range(1, parts)]

    barrier = pltpu.get_barrier_semaphore()
    each_peer(lambda peer: pl.semaphore_signal(barrier, inc=1, **at(tau, peer)))
    for part in other_parts:
        pl.semaphore_signal(barrier, inc=1, **at(part, me))
    load = pltpu.make_async_copy(t_hbm, tm, load_sem)
    load.start()

    lane = lax.broadcasted_iota(jnp.int32, (1, basis), 1)
    live = jnp.zeros((1, basis), F32)
    for a in range(atoms):
        hit = (lane >= a * FA) & (lane < a * FA + size_ref[a])
        live = live + one_hot(hit)
    atom_row = lax.broadcasted_iota(jnp.int32, (atoms, basis), 0)
    atom_lane = lax.broadcasted_iota(jnp.int32, (atoms, basis), 1) // FA
    spread = (one_hot(atom_row == atom_lane) * live).astype(BF)
    within = lax.broadcasted_iota(jnp.int32, (FA, basis), 0)
    live_rows = [one_hot(within < size_ref[me * row_atoms + a]) for a in range(row_atoms)]

    def factors(mask):
        return jnp.dot(mask.astype(F32).astype(BF), spread, preferred_element_type=F32)

    def masked_rows(rows_ref, mask_ref):
        f = factors(mask_ref[...])
        return jnp.concatenate(
            [
                rows_ref[a * FA : (a + 1) * FA, :].astype(F32) * (f[a : a + 1, :] * live_rows[a])
                for a in range(row_atoms)
            ],
            axis=0,
        )

    virtual = masked_rows(vg_ref, vm_ref)
    for x in range(parts):
        vown[x] = virtual[x * share : (x + 1) * share].astype(BF)
    vf[h_me, m_me, c_me, tau] = vown[tau]
    of[tau, h_me, m_me, c_me] = masked_rows(og_ref, om_ref).astype(BF)
    pl.semaphore_wait(barrier, n - 1 + parts - 1)

    def across(k, block, send_sem, recv_sem):
        hi = lax.rem(h_me + k, high)
        send(block, block, send_sem, recv_sem, tau, hi * 4 + m_me * 2 + c_me)

    mid_partner = h_me * 4 + (1 - m_me) * 2 + c_me
    core_partner = h_me * 4 + m_me * 2 + (1 - c_me)

    for part in other_parts:
        send(vown.at[part], vf.at[h_me, m_me, c_me, tau], v_send.at[0], v_recv.at[0], part, me)
    v_block = vf.at[h_me, m_me, c_me]
    o_block = of.at[tau, h_me, m_me, c_me]
    for k in range(1, high):
        across(k, o_block, o_send.at[0], o_recv.at[0])

    for a in range(row_atoms):
        factor[a] = factors(tmask_ref[:, a, :])

    def fill(table, piece, offset):
        count = table.shape[1]
        dst = lax.broadcasted_iota(jnp.int32, (1, count), 1)
        from_lane = (dst // LANES) * piece + dst % share + offset
        member = (dst % LANES) // share
        src = lax.broadcasted_iota(jnp.int32, (LANES, count), 0)
        for j in range(pack):
            wanted_lane = jnp.where(member == j, from_lane, -1)
            table[j * LANES : (j + 1) * LANES, :] = one_hot(src == wanted_lane).astype(BF)

    fill(perm_t, width, tau * share)

    def wait_v(stage, ref):
        wait_for(ref, v_recv.at[stage])

    wait_v(0, vown.at[pl.ds(0, parts - 1)])
    for k in range(1, high):
        across(k, v_block, v_send.at[1], v_recv.at[1])
    load.wait()

    def stack(pieces):
        chunks = pieces[0].shape[1] // LANES
        return jnp.concatenate(
            [
                jnp.concatenate([x[:, c * LANES : (c + 1) * LANES] for x in pieces], axis=1)
                for c in range(chunks)
            ],
            axis=0,
        )

    def tensor_step(q, carry):
        pieces = []
        for j in range(pack):
            values = []
            for r in range(GROUPS):
                p = j * groups + q * GROUPS + r
                f = [factor[a, pl.ds(p, 1), :] * live_rows[a] for a in range(row_atoms)]
                value = (tm[p].astype(F32) * jnp.concatenate(f, axis=0)).astype(BF)
                tm[p] = value
                values.append(value)
            pieces.append(jnp.concatenate(values, axis=0))
        moved = jnp.dot(stack(pieces), perm_t[...], preferred_element_type=F32).astype(BF)
        here = pl.ds(q * GROUPS, GROUPS)
        per = LANES // width
        for c in range(basis // LANES):
            for i in range(per):
                piece = moved[c * rows : (c + 1) * rows, i * LANES : (i + 1) * LANES]
                st[c * per + i, here] = piece.reshape(GROUPS, width, LANES)
        each_peer(
            lambda peer: send(st.at[peer, here], rt.at[me, here], t_send, t_recv, tau, peer)
        )
        return carry

    lax.fori_loop(0, 1, tensor_step, 0)
    wait_v(1, vf.at[pl.ds(0, high - 1), 0, 0])
    v_line = vf.at[:, m_me, c_me]
    send(v_line, v_line, v_send.at[2], v_recv.at[2], tau, mid_partner)
    wait_for(of.at[0, pl.ds(0, high - 1), 0, 0], o_recv.at[0])
    o_line = of.at[tau, :, m_me, c_me]
    send(o_line, o_line, o_send.at[1], o_recv.at[1], tau, mid_partner)

    lax.fori_loop(1, 2, tensor_step, 0)
    wait_v(2, v_line)
    v_plane = vf.at[:, :, c_me]
    send(v_plane, v_plane, v_send.at[3], v_recv.at[3], tau, core_partner)
    wait_for(o_line, o_recv.at[1])
    o_plane = of.at[tau, :, :, c_me]
    send(o_plane, o_plane, o_send.at[2], o_recv.at[2], tau, core_partner)

    lax.fori_loop(2, steps, tensor_step, 0)
    own_t = pltpu.make_async_copy(st.at[me], rt.at[me], own_sem.at[0])
    own_t.start()
    fill(perm_h, share, 0)

    wait_for(o_plane, o_recv.at[2])
    for part in other_parts:
        send(of.at[tau], of.at[tau], o_send.at[3], o_recv.at[3], part, me)
    wait_v(3, v_plane)
    mine = n * share
    for t in range(parts):
        vt[:, t * mine : (t + 1) * mine] = vf[:, :, :, t].reshape(mine, basis).T

    def half_step(q, carry):
        here = pl.ds(q * GROUPS, GROUPS)
        left = [
            tm[pl.ds(j * groups + q * GROUPS, GROUPS)].reshape(rows, basis) for j in range(pack)
        ]
        half = jnp.dot(
            jnp.concatenate(left, axis=0), vt[...], preferred_element_type=F32
        ).astype(BF)
        pieces = [half[j * rows : (j + 1) * rows] for j in range(pack)]
        moved = jnp.dot(stack(pieces), perm_h[...], preferred_element_type=F32).astype(BF)
        for c in range(basis // LANES):
            for i in range(pack):
                t, e = divmod(c * pack + i, n)
                piece = moved[c * rows : (c + 1) * rows, i * LANES : (i + 1) * LANES]
                sh[e, here, t] = piece.reshape(GROUPS, width, LANES)
        each_peer(
            lambda peer: send(sh.at[peer, here], rh.at[me, here], h_send, h_recv.at[q], tau, peer)
        )
        return carry

    lax.fori_loop(0, steps, half_step, 0)
    own_h = pltpu.make_async_copy(sh.at[me], rh.at[me], own_sem.at[1])
    own_h.start()

    pad_rows = csend.shape[1]
    slot = lax.broadcasted_iota(jnp.int32, (n * pad_rows, aux), 0)
    wanted = jnp.where(slot % pad_rows < owned, (slot // pad_rows) * owned + slot % pad_rows, -1)
    by_p = one_hot(wanted == owner_ref[...]).astype(BF)
    p_row = lax.broadcasted_iota(jnp.int32, (aux, aux), 0)
    p_col = lax.broadcasted_iota(jnp.int32, (aux, aux), 1)
    reorder = one_hot(p_row == (p_col % pack) * groups + p_col // pack).astype(BF)
    route[...] = jnp.dot(by_p, reorder, preferred_element_type=F32)
    chi[...] = jnp.zeros_like(chi)

    own_t.wait()
    wait_for(rt.at[pl.ds(0, n - 1)], t_recv)
    tiles = LANES // width

    def turn(g, carry):
        turned = rt[:, g].reshape(basis, LANES).T
        tm[pl.ds(g * tiles, tiles)] = turned.reshape(tiles, width, basis)
        return carry

    lax.fori_loop(0, groups, turn, 0)
    own_h.wait()
    wait_for(of.at[pl.ds(0, parts - 1)], o_recv.at[3])

    lanes = parts * GROUPS * LANES
    diag = one_hot(
        lax.broadcasted_iota(jnp.int32, (share, lanes), 0)
        == lax.broadcasted_iota(jnp.int32, (share, lanes), 1) % share
    )
    b_row = lax.broadcasted_iota(jnp.int32, (lanes, chi.shape[1]), 0)
    b_col = lax.broadcasted_iota(jnp.int32, (lanes, chi.shape[1]), 1)
    place = (
        b_row // (GROUPS * LANES) * aux
        + (b_row % LANES) // share * groups
        + (b_row // LANES) % GROUPS
    )

    def chi_step(q, carry):
        here = pl.ds(q * GROUPS, GROUPS)
        wait_for(rh.at[pl.ds(0, n - 1), here], h_recv.at[q])
        responses = []
        for t in range(parts):
            half = jnp.concatenate(
                [rh[:, q * GROUPS + r, t].reshape(basis, LANES) for r in range(GROUPS)], axis=1
            )
            responses.append(
                jnp.dot(
                    of[t].reshape(basis, basis), half, preferred_element_type=F32
                ).astype(BF)
            )
        response = jnp.concatenate(responses, axis=1)
        gather = one_hot(b_col == place + q * GROUPS)
        tile = 4 * tiles
        chi_rows = tile * width // share
        for k in range(groups // 4):
            left = tm[k * tile : (k + 1) * tile].reshape(tile * width, basis)
            both = jnp.dot(left, response, preferred_element_type=F32)
            traced = jnp.sum(both.reshape(chi_rows, share, lanes) * diag[None], axis=1)
            chi[k * chi_rows : (k + 1) * chi_rows, :] += jnp.dot(
                traced, gather, precision=lax.Precision.HIGHEST, preferred_element_type=F32
            )
        return carry

    lax.fori_loop(0, steps, chi_step, 0)

    routed = jnp.dot(
        route[...], chi[...], precision=lax.Precision.HIGHEST, preferred_element_type=F32
    )
    csend[...] = routed.reshape(csend.shape)
    crecv[me] = csend[me]
    each_peer(
        lambda peer: send(csend.at[peer], crecv.at[me], c_send.at[0], c_recv.at[0], tau, peer)
    )
    wait_for(crecv.at[pl.ds(0, n - 1)], c_recv.at[0])
    total = jnp.sum(crecv[...], axis=0) * (1.0 / basis)
    for t in range(parts):
        cmine[t, :, 0:aux] = total[:, t * aux : (t + 1) * aux]
    cother[tau] = cmine[tau]
    for part in other_parts:
        send(cmine.at[part], cother.at[tau], c_send.at[1], c_recv.at[1], part, me)
    wait_for(cother.at[pl.ds(0, parts - 1)], c_recv.at[1])
    out_ref[...] = jnp.sum(cother[...], axis=0)[:owned, :aux]

    wait_for(vown.at[pl.ds(0, parts - 1)], v_send.at[0])
    wait_for(vf.at[pl.ds(0, high - 1), 0, 0], v_send.at[1])
    wait_for(v_line, v_send.at[2])
    wait_for(v_plane, v_send.at[3])
    wait_for(of.at[0, pl.ds(0, high - 1), 0, 0], o_send.at[0])
    wait_for(o_line, o_send.at[1])
    wait_for(o_plane, o_send.at[2])
    wait_for(of.at[pl.ds(0, parts - 1)], o_send.at[3])
    wait_for(st.at[pl.ds(0, n - 1)], t_send)
    wait_for(sh.at[pl.ds(0, n - 1)], h_send)
    wait_for(csend.at[pl.ds(0, n - 1)], c_send.at[0])
    wait_for(cmine.at[pl.ds(0, parts - 1)], c_send.at[1])


def local(
    n,
    parts,
    three_center,
    tensor_mask,
    occupied_green,
    occupied_mask,
    virtual_green,
    virtual_mask,
    atom_size,
    auxiliary_owner,
):
    aux, width, basis = three_center.shape
    share = width // parts
    pack = LANES // share
    groups = aux // pack
    steps = groups // GROUPS
    wide = pack * LANES
    owned = aux // n
    pad_rows = -(-owned // 8) * 8
    cols = -(-parts * aux // LANES) * LANES
    one_cols = -(-aux // LANES) * LANES
    vmem = pl.BlockSpec(memory_space=pltpu.VMEM)
    sent_t = (n, groups, width, LANES)
    sent_h = (n, groups, parts, width, LANES)
    dma = pltpu.SemaphoreType.DMA
    return pl.pallas_call(
        functools.partial(kernel, n, parts),
        out_shape=jax.ShapeDtypeStruct((owned, aux), F32),
        in_specs=[pl.BlockSpec(memory_space=pl.ANY)]
        + [vmem] * 5
        + [pl.BlockSpec(memory_space=pltpu.SMEM), vmem],
        out_specs=vmem,
        scratch_shapes=[
            pltpu.VMEM((aux, width, basis), BF),
            pltpu.VMEM(sent_t, BF),
            pltpu.VMEM(sent_h, BF),
            pltpu.VMEM(sent_t, BF),
            pltpu.VMEM(sent_h, BF),
            pltpu.VMEM((parts, share, basis), BF),
            pltpu.VMEM((n // 4, 2, 2, parts, share, basis), BF),
            pltpu.VMEM((parts, n // 4, 2, 2, width, basis), BF),
            pltpu.VMEM((basis, basis), BF),
            pltpu.VMEM((wide, LANES // width * LANES), BF),
            pltpu.VMEM((wide, wide), BF),
            pltpu.VMEM((width // FA, aux, basis), F32),
            pltpu.VMEM((aux, cols), F32),
            pltpu.VMEM((n * pad_rows, aux), F32),
            pltpu.VMEM((n, pad_rows, cols), F32),
            pltpu.VMEM((n, pad_rows, cols), F32),
            pltpu.VMEM((parts, pad_rows, one_cols), F32),
            pltpu.VMEM((parts, pad_rows, one_cols), F32),
            dma,
            dma((2,)),
            dma((4,)),
            dma((4,)),
            dma((4,)),
            dma((4,)),
            dma,
            dma,
            dma,
            dma((steps,)),
            dma((2,)),
            dma((2,)),
        ],
        compiler_params=pltpu.CompilerParams(
            collective_id=0, has_side_effects=True, vmem_limit_bytes=61 * 1024 * 1024
        ),
    )(
        three_center,
        tensor_mask,
        occupied_green,
        occupied_mask,
        virtual_green,
        virtual_mask,
        atom_size,
        auxiliary_owner.reshape(1, aux),
    )


def solution(mesh):
    placed = (
        P(None, "basis", None),
        P(None, "basis", None),
        P(("tau", "basis"), None),
        P(("tau", "basis"), None),
        P(("tau", "basis"), None),
        P(("tau", "basis"), None),
        P(),
        P(),
    )
    return jax.shard_map(
        functools.partial(local, mesh.shape["basis"], mesh.shape["tau"]),
        mesh=mesh,
        in_specs=placed,
        out_specs=P(("tau", "basis"), None),
        check_vma=False,
    )
```

```python
import functools

import jax
import jax.numpy as jnp
from jax import lax
from jax.experimental import pallas as pl
from jax.experimental.pallas import tpu as pltpu
from jax.sharding import PartitionSpec as P

FA = 16
LANES = 128
GROUPS = 2
BF = jnp.bfloat16
F32 = jnp.float32


def wait_for(ref, sem):
    pltpu.make_async_copy(ref, ref, sem).wait()


def one_hot(cond):
    return jnp.where(cond, 1.0, 0.0).astype(F32)


def kernel(
    n,
    parts,
    t_hbm,
    tmask_ref,
    og_ref,
    om_ref,
    vg_ref,
    vm_ref,
    size_ref,
    owner_ref,
    out_ref,
    tm,
    st,
    sh,
    rt,
    rh,
    vown,
    vf,
    of,
    vt,
    perm_t,
    perm_h,
    factor,
    chi,
    route,
    csend,
    crecv,
    cmine,
    cother,
    load_sem,
    own_sem,
    v_send,
    v_recv,
    o_send,
    o_recv,
    t_send,
    t_recv,
    h_send,
    h_recv,
    c_send,
    c_recv,
):
    me = lax.axis_index("basis")
    tau = lax.axis_index("tau")
    aux, width, basis = tm.shape
    share = width // parts
    pack = LANES // share
    groups = aux // pack
    steps = groups // GROUPS
    atoms = basis // FA
    row_atoms = width // FA
    rows = GROUPS * width
    owned = aux // n
    high = n // 4
    h_me, l_me = me // 4, me % 4

    def peer_of(k):
        return lax.rem(me + n - k, n)

    def each_peer(body):
        def step(k, carry):
            body(peer_of(k))
            return carry

        lax.fori_loop(1, n, step, 0)

    def at(part, place):
        return dict(device_id=(part, place), device_id_type=pl.DeviceIdType.MESH)

    def send(src, dst, send_sem, recv_sem, part, place):
        pltpu.make_async_remote_copy(src, dst, send_sem, recv_sem, **at(part, place)).start()

    other_parts = [lax.rem(tau + k, parts) for k in range(1, parts)]

    def line_place(k):
        return lax.rem(h_me + k, high) * 4 + l_me

    line = [(part, line_place(k)) for part in other_parts for k in range(high)]
    line += [(tau, line_place(k)) for k in range(1, high)]
    layer = [h_me * 4 + lax.rem(me + k, 4) for k in range(1, 4)]

    barrier = pltpu.get_barrier_semaphore()
    each_peer(lambda peer: pl.semaphore_signal(barrier, inc=1, **at(tau, peer)))
    for part, place in line[: (parts - 1) * high]:
        pl.semaphore_signal(barrier, inc=1, **at(part, place))
    load = pltpu.make_async_copy(t_hbm, tm, load_sem)
    load.start()

    lane = lax.broadcasted_iota(jnp.int32, (1, basis), 1)
    live = jnp.zeros((1, basis), F32)
    for a in range(atoms):
        hit = (lane >= a * FA) & (lane < a * FA + size_ref[a])
        live = live + one_hot(hit)
    atom_row = lax.broadcasted_iota(jnp.int32, (atoms, basis), 0)
    atom_lane = lax.broadcasted_iota(jnp.int32, (atoms, basis), 1) // FA
    spread = (one_hot(atom_row == atom_lane) * live).astype(BF)
    within = lax.broadcasted_iota(jnp.int32, (FA, basis), 0)
    live_rows = [one_hot(within < size_ref[me * row_atoms + a]) for a in range(row_atoms)]

    def factors(mask):
        return jnp.dot(mask.astype(F32).astype(BF), spread, preferred_element_type=F32)

    def masked_rows(rows_ref, mask_ref):
        f = factors(mask_ref[...])
        return jnp.concatenate(
            [
                rows_ref[a * FA : (a + 1) * FA, :].astype(F32) * (f[a : a + 1, :] * live_rows[a])
                for a in range(row_atoms)
            ],
            axis=0,
        )

    virtual = masked_rows(vg_ref, vm_ref)
    for x in range(parts):
        vown[x] = virtual[x * share : (x + 1) * share].astype(BF)
    vf[l_me, h_me * parts + tau] = vown[tau]
    of[tau, l_me, h_me] = masked_rows(og_ref, om_ref).astype(BF)
    pl.semaphore_wait(barrier, n - 1 + (parts - 1) * high)

    v_block = vf.at[l_me, h_me * parts + tau]
    for part, place in line:
        send(vown.at[part], v_block, v_send.at[0], v_recv.at[0], part, place)
    o_block = of.at[tau, l_me, h_me]
    for part, place in line[(parts - 1) * high :]:
        send(o_block, o_block, o_send.at[0], o_recv.at[0], part, place)

    for a in range(row_atoms):
        factor[a] = factors(tmask_ref[:, a, :])

    def fill(table, piece, offset):
        count = table.shape[1]
        dst = lax.broadcasted_iota(jnp.int32, (1, count), 1)
        from_lane = (dst // LANES) * piece + dst % share + offset
        member = (dst % LANES) // share
        src = lax.broadcasted_iota(jnp.int32, (LANES, count), 0)
        for j in range(pack):
            wanted_lane = jnp.where(member == j, from_lane, -1)
            table[j * LANES : (j + 1) * LANES, :] = one_hot(src == wanted_lane).astype(BF)

    fill(perm_t, width, tau * share)

    load.wait()

    def stack(pieces):
        chunks = pieces[0].shape[1] // LANES
        return jnp.concatenate(
            [
                jnp.concatenate([x[:, c * LANES : (c + 1) * LANES] for x in pieces], axis=1)
                for c in range(chunks)
            ],
            axis=0,
        )

    def tensor_step(q, carry):
        pieces = []
        for j in range(pack):
            values = []
            for r in range(GROUPS):
                p = j * groups + q * GROUPS + r
                f = [factor[a, pl.ds(p, 1), :] * live_rows[a] for a in range(row_atoms)]
                value = (tm[p].astype(F32) * jnp.concatenate(f, axis=0)).astype(BF)
                tm[p] = value
                values.append(value)
            pieces.append(jnp.concatenate(values, axis=0))
        moved = jnp.dot(stack(pieces), perm_t[...], preferred_element_type=F32).astype(BF)
        here = pl.ds(q * GROUPS, GROUPS)
        per = LANES // width
        for c in range(basis // LANES):
            for i in range(per):
                piece = moved[c * rows : (c + 1) * rows, i * LANES : (i + 1) * LANES]
                st[c * per + i, here] = piece.reshape(GROUPS, width, LANES)
        each_peer(
            lambda peer: send(st.at[peer, here], rt.at[me, here], t_send, t_recv, tau, peer)
        )
        return carry

    lax.fori_loop(0, 1, tensor_step, 0)
    wait_for(vf.at[0, pl.ds(0, parts * high - 1)], v_recv.at[0])
    v_line = vf.at[l_me]
    for place in layer:
        send(v_line, v_line, v_send.at[1], v_recv.at[1], tau, place)
    wait_for(of.at[0, 0, pl.ds(0, high - 1)], o_recv.at[0])
    o_line = of.at[tau, l_me]
    for place in layer:
        send(o_line, o_line, o_send.at[1], o_recv.at[1], tau, place)

    lax.fori_loop(1, steps, tensor_step, 0)
    own_t = pltpu.make_async_copy(st.at[me], rt.at[me], own_sem.at[0])
    own_t.start()
    fill(perm_h, share, 0)

    wait_for(vf.at[pl.ds(0, 3)], v_recv.at[1])
    mine = n * share
    for t in range(parts):
        ordered = [vf[:, h * parts + t].reshape(4 * share, basis) for h in range(high)]
        vt[:, t * mine : (t + 1) * mine] = jnp.concatenate(ordered, axis=0).T

    def half_step(q, carry):
        here = pl.ds(q * GROUPS, GROUPS)
        left = [
            tm[pl.ds(j * groups + q * GROUPS, GROUPS)].reshape(rows, basis) for j in range(pack)
        ]
        half = jnp.dot(
            jnp.concatenate(left, axis=0), vt[...], preferred_element_type=F32
        ).astype(BF)
        pieces = [half[j * rows : (j + 1) * rows] for j in range(pack)]
        moved = jnp.dot(stack(pieces), perm_h[...], preferred_element_type=F32).astype(BF)
        for c in range(basis // LANES):
            for i in range(pack):
                t, e = divmod(c * pack + i, n)
                piece = moved[c * rows : (c + 1) * rows, i * LANES : (i + 1) * LANES]
                sh[e, here, t] = piece.reshape(GROUPS, width, LANES)
        each_peer(
            lambda peer: send(sh.at[peer, here], rh.at[me, here], h_send, h_recv.at[q], tau, peer)
        )
        return carry

    lax.fori_loop(0, steps, half_step, 0)
    own_h = pltpu.make_async_copy(sh.at[me], rh.at[me], own_sem.at[1])
    own_h.start()
    wait_for(of.at[0, pl.ds(0, 3)], o_recv.at[1])
    for part in other_parts:
        send(of.at[tau], of.at[tau], o_send.at[2], o_recv.at[2], part, me)

    pad_rows = csend.shape[1]
    slot = lax.broadcasted_iota(jnp.int32, (n * pad_rows, aux), 0)
    wanted = jnp.where(slot % pad_rows < owned, (slot // pad_rows) * owned + slot % pad_rows, -1)
    by_p = one_hot(wanted == owner_ref[...]).astype(BF)
    p_row = lax.broadcasted_iota(jnp.int32, (aux, aux), 0)
    p_col = lax.broadcasted_iota(jnp.int32, (aux, aux), 1)
    reorder = one_hot(p_row == (p_col % pack) * groups + p_col // pack).astype(BF)
    route[...] = jnp.dot(by_p, reorder, preferred_element_type=F32)
    chi[...] = jnp.zeros_like(chi)

    own_t.wait()
    wait_for(rt.at[pl.ds(0, n - 1)], t_recv)
    tiles = LANES // width

    def turn(g, carry):
        turned = rt[:, g].reshape(basis, LANES).T
        tm[pl.ds(g * tiles, tiles)] = turned.reshape(tiles, width, basis)
        return carry

    lax.fori_loop(0, groups, turn, 0)
    own_h.wait()
    wait_for(of.at[pl.ds(0, parts - 1)], o_recv.at[2])

    lanes = parts * GROUPS * LANES
    diag = one_hot(
        lax.broadcasted_iota(jnp.int32, (share, lanes), 0)
        == lax.broadcasted_iota(jnp.int32, (share, lanes), 1) % share
    )
    b_row = lax.broadcasted_iota(jnp.int32, (lanes, chi.shape[1]), 0)
    b_col = lax.broadcasted_iota(jnp.int32, (lanes, chi.shape[1]), 1)
    place = (
        b_row // (GROUPS * LANES) * aux
        + (b_row % LANES) // share * groups
        + (b_row // LANES) % GROUPS
    )

    def chi_step(q, carry):
        here = pl.ds(q * GROUPS, GROUPS)
        wait_for(rh.at[pl.ds(0, n - 1), here], h_recv.at[q])
        responses = []
        for t in range(parts):
            half = jnp.concatenate(
                [rh[:, q * GROUPS + r, t].reshape(basis, LANES) for r in range(GROUPS)], axis=1
            )
            occupied = jnp.concatenate(
                [of[t, :, h].reshape(4 * width, basis) for h in range(high)], axis=0
            )
            responses.append(
                jnp.dot(occupied, half, preferred_element_type=F32).astype(BF)
            )
        response = jnp.concatenate(responses, axis=1)
        gather = one_hot(b_col == place + q * GROUPS)
        tile = 4 * tiles
        chi_rows = tile * width // share
        for k in range(groups // 4):
            left = tm[k * tile : (k + 1) * tile].reshape(tile * width, basis)
            both = jnp.dot(left, response, preferred_element_type=F32)
            traced = jnp.sum(both.reshape(chi_rows, share, lanes) * diag[None], axis=1)
            chi[k * chi_rows : (k + 1) * chi_rows, :] += jnp.dot(
                traced, gather, precision=lax.Precision.HIGHEST, preferred_element_type=F32
            )
        return carry

    lax.fori_loop(0, steps, chi_step, 0)

    routed = jnp.dot(
        route[...], chi[...], precision=lax.Precision.HIGHEST, preferred_element_type=F32
    )
    csend[...] = routed.reshape(csend.shape)
    crecv[me] = csend[me]
    each_peer(
        lambda peer: send(csend.at[peer], crecv.at[me], c_send.at[0], c_recv.at[0], tau, peer)
    )
    wait_for(crecv.at[pl.ds(0, n - 1)], c_recv.at[0])
    total = jnp.sum(crecv[...], axis=0) * (1.0 / basis)
    for t in range(parts):
        cmine[t, :, 0:aux] = total[:, t * aux : (t + 1) * aux]
    cother[tau] = cmine[tau]
    for part in other_parts:
        send(cmine.at[part], cother.at[tau], c_send.at[1], c_recv.at[1], part, me)
    wait_for(cother.at[pl.ds(0, parts - 1)], c_recv.at[1])
    out_ref[...] = jnp.sum(cother[...], axis=0)[:owned, :aux]

    wait_for(vf.at[0, pl.ds(0, parts * high - 1)], v_send.at[0])
    wait_for(vf.at[pl.ds(0, 3)], v_send.at[1])
    wait_for(of.at[0, 0, pl.ds(0, high - 1)], o_send.at[0])
    wait_for(of.at[0, pl.ds(0, 3)], o_send.at[1])
    wait_for(of.at[pl.ds(0, parts - 1)], o_send.at[2])
    wait_for(st.at[pl.ds(0, n - 1)], t_send)
    wait_for(sh.at[pl.ds(0, n - 1)], h_send)
    wait_for(csend.at[pl.ds(0, n - 1)], c_send.at[0])
    wait_for(cmine.at[pl.ds(0, parts - 1)], c_send.at[1])


def local(
    n,
    parts,
    three_center,
    tensor_mask,
    occupied_green,
    occupied_mask,
    virtual_green,
    virtual_mask,
    atom_size,
    auxiliary_owner,
):
    aux, width, basis = three_center.shape
    share = width // parts
    pack = LANES // share
    groups = aux // pack
    steps = groups // GROUPS
    wide = pack * LANES
    owned = aux // n
    pad_rows = -(-owned // 8) * 8
    cols = -(-parts * aux // LANES) * LANES
    one_cols = -(-aux // LANES) * LANES
    vmem = pl.BlockSpec(memory_space=pltpu.VMEM)
    sent_t = (n, groups, width, LANES)
    sent_h = (n, groups, parts, width, LANES)
    dma = pltpu.SemaphoreType.DMA
    return pl.pallas_call(
        functools.partial(kernel, n, parts),
        out_shape=jax.ShapeDtypeStruct((owned, aux), F32),
        in_specs=[pl.BlockSpec(memory_space=pl.ANY)]
        + [vmem] * 5
        + [pl.BlockSpec(memory_space=pltpu.SMEM), vmem],
        out_specs=vmem,
        scratch_shapes=[
            pltpu.VMEM((aux, width, basis), BF),
            pltpu.VMEM(sent_t, BF),
            pltpu.VMEM(sent_h, BF),
            pltpu.VMEM(sent_t, BF),
            pltpu.VMEM(sent_h, BF),
            pltpu.VMEM((parts, share, basis), BF),
            pltpu.VMEM((4, n // 4 * parts, share, basis), BF),
            pltpu.VMEM((parts, 4, n // 4, width, basis), BF),
            pltpu.VMEM((basis, basis), BF),
            pltpu.VMEM((wide, LANES // width * LANES), BF),
            pltpu.VMEM((wide, wide), BF),
            pltpu.VMEM((width // FA, aux, basis), F32),
            pltpu.VMEM((aux, cols), F32),
            pltpu.VMEM((n * pad_rows, aux), F32),
            pltpu.VMEM((n, pad_rows, cols), F32),
            pltpu.VMEM((n, pad_rows, cols), F32),
            pltpu.VMEM((parts, pad_rows, one_cols), F32),
            pltpu.VMEM((parts, pad_rows, one_cols), F32),
            dma,
            dma((2,)),
            dma((2,)),
            dma((2,)),
            dma((3,)),
            dma((3,)),
            dma,
            dma,
            dma,
            dma((steps,)),
            dma((2,)),
            dma((2,)),
        ],
        compiler_params=pltpu.CompilerParams(
            collective_id=0, has_side_effects=True, vmem_limit_bytes=61 * 1024 * 1024
        ),
    )(
        three_center,
        tensor_mask,
        occupied_green,
        occupied_mask,
        virtual_green,
        virtual_mask,
        atom_size,
        auxiliary_owner.reshape(1, aux),
    )


def solution(mesh):
    placed = (
        P(None, "basis", None),
        P(None, "basis", None),
        P(("tau", "basis"), None),
        P(("tau", "basis"), None),
        P(("tau", "basis"), None),
        P(("tau", "basis"), None),
        P(),
        P(),
    )
    return jax.shard_map(
        functools.partial(local, mesh.shape["basis"], mesh.shape["tau"]),
        mesh=mesh,
        in_specs=placed,
        out_specs=P(("tau", "basis"), None),
        check_vma=False,
    )
```
